32 devices in a mesh: inp: 8 (over y, x, core), out: 4 (over z).
Axes of the slice: x: 2, y: 2, z: 4, core: 2. Of those that a mesh axis runs over, the one named last changes fastest.
Arguments:
- tokens: bfloat16 [1536, 8192], P('out', 'inp'), may hold values from -6 to 6
- weight: bfloat16 [8192, 28672], P('inp', 'out'), may hold values from -0.0625 to 0.0625
- adapter_a: bfloat16 [4, 8192, 16], P(None, 'inp'), as said below
- adapter_b: bfloat16 [4, 16, 28672], P(None, None, 'out'), may hold values from -1 to 1
- magnitude: float32 [4, 28672], P(None, 'out'), may hold values from 0.5 to 2
- row_tenant: int32 [1536], replicated, may hold values from 0 to 3, as said below
- tenant_count: int32 [4], replicated, may hold values from 1 to 640, as said below
- grad_out: bfloat16 [1536, 28672], P('inp', 'out'), may hold values from -6 to 6
Outputs:
- output: bfloat16 [1536, 28672], P('inp', 'out')
- grad_tokens: bfloat16 [1536, 8192], P('out', 'inp')
- grad_a: float32 [4, 8192, 16], P(None, 'inp')
- grad_b: float32 [4, 16, 28672], P(None, None, 'out')
- grad_mag: float32 [4, 28672], P(None, 'out')
The draws below stay inside these ranges and needn't reach their ends.
Inputs may be any that keep to these rules, and one draw needn't show every extreme that they name: `row_tenant`: rows are in ascending tenant order; each tenant owns a whole number of consecutive blocks of 128 rows, at least one; tenant 0 owns exactly one block, the last tenant owns the most blocks, and no tenant owns more than (5) blocks. A tenant's live rows are the first tenant_count of its rows; the count exceeds its rows minus 128. `adapter_a`: every entry lies within 6 / sqrt(8192) of zero.
All inputs are finite; a program needn't handle non-finite values.
Results may differ from the reference program's by a relative error of at most 0.0049.
Values may be sent and summed in bfloat16 or wider, within the bound.
A program may use at most 192 MiB of HBM per device.

```python
import math
import jax
import jax.numpy as jnp
from jax import lax

D = 8192
F = 28672
RANK = 16
TENANTS = 4
ROWBLOCK = 128
TOKENS = 1536
BLOCKS = 12


def block_owners(key):
    extra_total = BLOCKS - TENANTS
    last_extra = extra_total // 2
    rest_extra = extra_total - last_extra
    middle_slots = 1 + jnp.arange((TENANTS - 2) * last_extra, dtype=jnp.int32) // max(last_extra, 1)
    shuffled = jax.random.permutation(key, middle_slots)
    chosen = shuffled[:rest_extra].astype(jnp.int32)
    last_blocks = jnp.full((last_extra,), TENANTS - 1, dtype=jnp.int32)
    owners = jnp.concatenate([jnp.arange(TENANTS, dtype=jnp.int32), chosen, last_blocks])
    return jnp.sort(owners).astype(jnp.int32)


def draw_row_tenant(key, part):
    owners = block_owners(key)
    return jnp.repeat(owners, ROWBLOCK).astype(jnp.int32)


def draw_tenant_count(key, part):
    owners = block_owners(key)
    key = jax.random.fold_in(key, 7)
    tenant_ids = jnp.arange(TENANTS, dtype=jnp.int32)
    allotted = jnp.sum((owners[None, :] == tenant_ids[:, None]).astype(jnp.int32), axis=1) * ROWBLOCK
    shortfall = jax.random.randint(key, (TENANTS,), 0, ROWBLOCK).astype(jnp.int32)
    shortfall = jnp.where(tenant_ids == 0, ROWBLOCK - 1, shortfall)
    shortfall = jnp.where(tenant_ids == TENANTS - 1, 0, shortfall)
    return (allotted - shortfall).astype(jnp.int32)


def draw_adapter_a(key, part):
    key = jax.random.fold_in(key, 11)
    shared_key, own_key = jax.random.split(key)
    common = 1.0
    shared = jnp.clip(jax.random.normal(shared_key, (TENANTS, D, 1), jnp.float32), -4.0, 4.0)
    own = jnp.clip(jax.random.normal(own_key, (TENANTS, D, RANK), jnp.float32), -4.0, 4.0)
    factor = 1.0 / math.sqrt(D * (1.0 + common))
    return ((shared + own) * factor).astype(jnp.bfloat16)


def level_of(rng, shape, cuts, smallest, high):
    loudness = 1.0
    for dim, shards_of in cuts:
        heights = jax.random.uniform(jax.random.fold_in(jax.random.fold_in(rng, 6), dim), (shards_of,), jnp.float32, smallest / len(cuts), high / len(cuts))
        loudness = loudness * jnp.repeat(jnp.exp(heights), shape[dim] // shards_of).reshape((-1,) + (1,) * (len(shape) - 1 - dim))
    return loudness


def centred(rng, shape, deviation, reach, cuts=(), held_as=jnp.bfloat16):
    drawn = jax.random.normal(rng, shape, jnp.float32) * deviation
    if len(cuts) > 0:
        drawn = level_of(rng, shape, cuts, -0.22, 0.18) * drawn
    return jnp.clip(drawn, min=-reach, max=reach).astype(held_as)


def setup_inputs(seed: int = 0) -> dict:
    streams_of = jax.random.split(jax.random.key(seed), 9)
    tokens = centred(streams_of[0], (TOKENS, D), 1.0, 6.0, ((0, 4), (1, 8)))
    weight = centred(streams_of[1], (D, F), D ** -0.5, 0.0625, ((0, 8), (1, 4)))
    adapter_a = draw_adapter_a(jax.random.fold_in(streams_of[8], 71), 0)
    adapter_b = centred(streams_of[3], (TENANTS, RANK, F), (2 * RANK) ** -0.5, 1.0, ((2, 4),))
    magnitude = jnp.clip(jnp.exp(math.log(2.0) - 1.3862944 * jax.random.uniform(streams_of[4], (TENANTS, F), jnp.float32) ** level_of(streams_of[4], (TENANTS, F), ((1, 4),), -0.2, 0.2)), 0.5, 2.0)
    row_tenant = draw_row_tenant(jax.random.fold_in(streams_of[8], 71), 0)
    tenant_count = draw_tenant_count(jax.random.fold_in(streams_of[8], 71), 0)
    grad_out = centred(streams_of[7], (TOKENS, F), 1.0, 6.0, ((0, 8), (1, 4)))
    return {"tokens": tokens, "weight": weight, "adapter_a": adapter_a, "adapter_b": adapter_b, "magnitude": magnitude, "row_tenant": row_tenant, "tenant_count": tenant_count, "grad_out": grad_out}


epsilon = 1e-06

def mask_table(row_tenant, tenant_count):
    row_total = row_tenant.shape[0]
    tenant_ids = jnp.arange(tenant_count.shape[0], dtype=jnp.int32)
    onehot = (row_tenant[:, None] == tenant_ids[None, :]).astype(jnp.int32)
    offsets = lax.optimization_barrier(jnp.sum((row_tenant[:, None] < tenant_ids[None, :]).astype(jnp.int32), axis=0))
    first_row = lax.optimization_barrier(jnp.sum(onehot * offsets[None, :], axis=1))
    row_limit = lax.optimization_barrier(jnp.sum(onehot * tenant_count[None, :], axis=1))
    position = jnp.arange(row_total, dtype=jnp.int32) - first_row
    alive = (position < row_limit).astype(jnp.int32)
    return (onehot * alive[:, None]).astype(jnp.float32)

def reference(tokens, weight, adapter_a, adapter_b, magnitude, row_tenant, tenant_count, grad_out):
    highest = lax.Precision.HIGHEST
    contract_rows = (((0,), (0,)), ((), ()))
    contract_cols = (((1,), (1,)), ((), ()))
    live_table = mask_table(row_tenant, tenant_count)
    slot_mask = jnp.repeat(live_table, RANK, axis=1)
    a_columns = jnp.transpose(adapter_a, (1, 0, 2)).reshape(D, TENANTS * RANK)
    b_rows = adapter_b.reshape(TENANTS * RANK, F)
    low_in = jnp.dot(tokens, a_columns, preferred_element_type=jnp.float32) * slot_mask
    squares = lax.optimization_barrier(jnp.sum(jnp.square(weight.astype(jnp.float32)), axis=0))
    weight_adapt = lax.dot_general(weight, a_columns, contract_rows, preferred_element_type=jnp.float32)
    b_float = adapter_b.astype(jnp.float32)
    cross_term = jnp.einsum('jtr,trj->tj', weight_adapt.reshape(F, TENANTS, RANK), b_float, precision=highest)
    a_float = adapter_a.astype(jnp.float32)
    gram_whole = jnp.einsum('tkr,tks->trs', a_float, a_float, precision=highest)
    quadratic = jnp.einsum('trj,trs,tsj->tj', b_float, gram_whole, b_float, precision=highest)
    norm2 = squares[None, :] + 2.0 * cross_term + quadratic
    inverse = 1.0 / jnp.sqrt(norm2 + epsilon)
    col_scale = magnitude * inverse
    values = jnp.dot(tokens, weight, preferred_element_type=jnp.float32) + jnp.dot(low_in, b_rows.astype(jnp.float32), precision=highest)
    row_scale = jnp.dot(live_table, col_scale, precision=highest)
    output = (row_scale * values).astype(jnp.bfloat16)
    upstream = grad_out.astype(jnp.float32)
    scaled = (upstream * row_scale).astype(jnp.bfloat16)
    grad_mag = lax.dot_general(live_table, upstream * values, contract_rows, precision=highest) * inverse
    low_bf = low_in.astype(jnp.bfloat16)
    grad_b = lax.dot_general(low_bf, scaled, contract_rows, preferred_element_type=jnp.float32).reshape(TENANTS, RANK, F)
    back_sum = lax.dot_general(scaled, b_rows, contract_cols, preferred_element_type=jnp.float32) * slot_mask
    grad_main = lax.dot_general(scaled, weight, contract_cols, preferred_element_type=jnp.float32)
    grad_tokens = (grad_main + jnp.dot(back_sum, a_columns.astype(jnp.float32).T, precision=highest)).astype(jnp.bfloat16)
    grad_flat = lax.dot_general(tokens.astype(jnp.float32), back_sum, contract_rows, precision=highest)
    grad_a = jnp.transpose(grad_flat.reshape(D, TENANTS, RANK), (1, 0, 2))
    return (output, grad_tokens, grad_a, grad_b, grad_mag)
```

```python
import functools

import jax
import jax.numpy as jnp
from jax import lax
from jax.experimental import pallas as pl
from jax.experimental.pallas import tpu as pltpu
from jax.sharding import PartitionSpec as P

epsilon = 1e-06


def mask_table(row_tenant, tenant_count):
    row_total = row_tenant.shape[0]
    tenant_ids = jnp.arange(tenant_count.shape[0], dtype=jnp.int32)
    onehot = (row_tenant[:, None] == tenant_ids[None, :]).astype(jnp.int32)
    offsets = jnp.sum((row_tenant[:, None] < tenant_ids[None, :]).astype(jnp.int32), axis=0)
    first_row = jnp.sum(onehot * offsets[None, :], axis=1)
    row_limit = jnp.sum(onehot * tenant_count[None, :], axis=1)
    position = jnp.arange(row_total, dtype=jnp.int32) - first_row
    alive = (position < row_limit).astype(jnp.int32)
    return (onehot * alive[:, None]).astype(jnp.float32)


def shards(tokens, weight, adapter_a, adapter_b, magnitude, row_tenant, tenant_count, grad_out):
    highest = lax.Precision.HIGHEST
    contract_rows = (((0,), (0,)), ((), ()))
    contract_cols = (((1,), (1,)), ((), ()))
    tenants, d_local, rank_width = adapter_a.shape
    f_local = weight.shape[1]
    row_total = row_tenant.shape[0]
    inp_rows = row_total // lax.axis_size("inp")
    out_rows = row_total // lax.axis_size("out")
    live_table = mask_table(row_tenant, tenant_count)
    slot_mask = jnp.repeat(live_table, rank_width, axis=1)
    a_columns = jnp.transpose(adapter_a, (1, 0, 2)).reshape(d_local, tenants * rank_width)
    b_rows = adapter_b.reshape(tenants * rank_width, f_local)
    gathered = lax.all_gather(tokens, "out", axis=0, tiled=True)
    low_part = jnp.dot(gathered, a_columns, preferred_element_type=jnp.float32) * slot_mask
    low_in = lax.psum(low_part, "inp")
    squares = jnp.sum(jnp.square(weight.astype(jnp.float32)), axis=0)
    weight_adapt = lax.dot_general(
        weight, a_columns, contract_rows, preferred_element_type=jnp.float32
    )
    b_float = adapter_b.astype(jnp.float32)
    cross_term = jnp.einsum(
        "jtr,trj->tj",
        weight_adapt.reshape(f_local, tenants, rank_width),
        b_float,
        precision=highest,
    )
    a_float = adapter_a.astype(jnp.float32)
    gram_local = jnp.einsum("tkr,tks->trs", a_float, a_float, precision=highest)
    quadratic = jnp.einsum("trj,trs,tsj->tj", b_float, gram_local, b_float, precision=highest)
    partial_norm = squares[None, :] + 2.0 * cross_term + quadratic
    norm2 = lax.psum(partial_norm, "inp")
    inverse = 1.0 / jnp.sqrt(norm2 + epsilon)
    col_scale = magnitude * inverse
    own_start = lax.axis_index("inp") * inp_rows
    frozen_rows = lax.psum_scatter(
        jnp.dot(gathered, weight, preferred_element_type=jnp.float32),
        "inp",
        scatter_dimension=0,
        tiled=True,
    )
    own_low = lax.dynamic_slice_in_dim(low_in, own_start, inp_rows, 0)
    values = frozen_rows + jnp.dot(own_low, b_rows.astype(jnp.float32), precision=highest)
    own_live = lax.dynamic_slice_in_dim(live_table, own_start, inp_rows, 0)
    row_scale = jnp.dot(own_live, col_scale, precision=highest)
    output = (row_scale * values).astype(jnp.bfloat16)
    upstream = grad_out.astype(jnp.float32)
    scaled = (upstream * row_scale).astype(jnp.bfloat16)
    mag_part = lax.dot_general(own_live, upstream * values, contract_rows, precision=highest)
    grad_mag = lax.psum(mag_part, "inp") * inverse
    low_bf = low_in.astype(jnp.bfloat16)
    grad_piece = lax.all_gather(scaled, "inp", axis=0, tiled=True)
    b_grad = lax.dot_general(low_bf, grad_piece, contract_rows, preferred_element_type=jnp.float32)
    back_piece = lax.dot_general(
        grad_piece, b_rows, contract_cols, preferred_element_type=jnp.float32
    )
    input_piece = lax.dot_general(
        grad_piece, weight, contract_cols, preferred_element_type=jnp.float32
    )
    back_part = back_piece
    back_part = back_part * slot_mask
    a_cols_float = a_columns.astype(jnp.float32)
    gathered_float = gathered.astype(jnp.float32)
    back_sum = lax.psum(back_part, "out")
    grad_flat = lax.dot_general(gathered_float, back_sum, contract_rows, precision=highest)
    out_start = lax.axis_index("out") * out_rows
    back_rows = lax.dynamic_slice_in_dim(back_sum, out_start, out_rows, 0)
    grad_rows = lax.psum_scatter(input_piece, "out", scatter_dimension=0, tiled=True)
    grad_tokens = (grad_rows + jnp.dot(back_rows, a_cols_float.T, precision=highest)).astype(
        jnp.bfloat16
    )
    grad_a = jnp.transpose(grad_flat.reshape(d_local, tenants, rank_width), (1, 0, 2))
    grad_b = b_grad.reshape(tenants, rank_width, f_local)
    return (output, grad_tokens, grad_a, grad_b, grad_mag)


TILE = 512
SLOTS = ((0, 0), (0, 1), (1, 0), (1, 1))


def forward_kernel(count, places, tok_ref, low_ref, w_ref, b_ref, *rest):
    outs, scratch = rest[-count - 1 : -1], rest[-1]
    piece = outs[0].shape[0]
    total = jnp.dot(tok_ref[...], w_ref[...], preferred_element_type=jnp.float32)
    total = total + jnp.dot(low_ref[...], b_ref[...], preferred_element_type=jnp.float32)
    scratch[...] = total.astype(jnp.bfloat16)
    for slot, out in enumerate(outs):
        start = pl.multiple_of(places[slot], 32)
        out[...] = scratch[pl.ds(start, piece), :]


def partial_values(places, tokens, low, weight, b_rows, piece, first, last, after, filled):
    rows, depth = tokens.shape
    width = weight.shape[1]
    rank = low.shape[1]
    count = rows // piece
    extra = [*after, *filled]
    aliases = {5 + len(after) + k: k for k in range(len(filled))}
    return pl.pallas_call(
        functools.partial(forward_kernel, count),
        input_output_aliases=aliases,
        grid_spec=pltpu.PrefetchScalarGridSpec(
            num_scalar_prefetch=1,
            grid=(last - first,),
            in_specs=[
                pl.BlockSpec((rows, depth), lambda j, s: (0, 0)),
                pl.BlockSpec((rows, rank), lambda j, s: (0, 0)),
                pl.BlockSpec((depth, TILE), lambda j, s: (0, j + first)),
                pl.BlockSpec((rank, TILE), lambda j, s: (0, j + first)),
            ]
            + [pl.BlockSpec(memory_space=pl.ANY)] * len(extra),
            out_specs=[pl.BlockSpec((piece, TILE), lambda j, s: (0, j + first))] * count,
            scratch_shapes=[pltpu.VMEM((rows, TILE), jnp.bfloat16)],
        ),
        out_shape=[jax.ShapeDtypeStruct((piece, width), jnp.bfloat16)] * count,
        compiler_params=pltpu.CompilerParams(vmem_limit_bytes=48 * 2**20),
        cost_estimate=pl.CostEstimate(
            flops=rows * (depth + rank) * width,
            bytes_accessed=depth * width + rows * width + rows * depth,
            transcendentals=0,
        ),
    )(places, tokens, low, weight, b_rows, *extra)


def backward_kernel(count, final, places, *refs):
    grads, parts = refs[:count], refs[count : 2 * count]
    w_ref, b_ref, scale_ref, live_ref, live_t_ref, low_t_ref, mask_ref, a_ref = refs[
        2 * count : 2 * count + 8
    ]
    tok_out, back_out, gradb_out, mag_out = refs[-7:-3] if final else refs[-6:-2]
    scaled, product = refs[-2:]
    total = refs[-3] if final else tok_out
    step = pl.program_id(0)
    piece = grads[0].shape[0]
    contract_cols = (((1,), (1,)), ((), ()))

    @pl.when(step == 0)
    def _():
        if final:
            total[...] = refs[2 * count + 8][...]
            back_out[...] = refs[2 * count + 9][...]
        else:
            total[...] = jnp.zeros_like(total)
            back_out[...] = jnp.zeros_like(back_out)

    col_scale = scale_ref[...]
    high = col_scale.astype(jnp.bfloat16).astype(jnp.float32)
    both = jnp.concatenate([high, col_scale - high], axis=0).astype(jnp.bfloat16)
    for slot in range(count):
        start = pl.multiple_of(places[slot], 32)
        here = pl.ds(start, piece)
        row_scale = jnp.dot(live_ref[here, :], both, preferred_element_type=jnp.float32)
        upstream = grads[slot][...].astype(jnp.float32)
        scaled[here, :] = (upstream * row_scale).astype(jnp.bfloat16)
        product[here, :] = (upstream * parts[slot][...].astype(jnp.float32)).astype(jnp.bfloat16)
    back_out[...] += lax.dot_general(
        scaled[...], b_ref[...], contract_cols, preferred_element_type=jnp.float32
    )
    gradb_out[...] = jnp.dot(low_t_ref[...], scaled[...], preferred_element_type=jnp.float32)
    mag_out[...] = jnp.dot(live_t_ref[...], product[...], preferred_element_type=jnp.float32)
    total[...] += lax.dot_general(
        scaled[...], w_ref[...], contract_cols, preferred_element_type=jnp.float32
    )

    if not final:
        return

    @pl.when(step == pl.num_programs(0) - 1)
    def _():
        back = back_out[...] * mask_ref[...]
        back_out[...] = back
        adapter = lax.dot_general(
            back.astype(jnp.bfloat16), a_ref[...], contract_cols, preferred_element_type=jnp.float32
        )
        tok_out[...] = (total[...] + adapter).astype(jnp.bfloat16)


def backward_parts(
    places, grads, parts, weight, b_rows, scale8, live16, live_t, low_t, mask, a_cols, first, last, sums, after
):
    final = len(sums) > 0
    count = len(grads)
    piece, width = grads[0].shape
    rows = piece * count
    depth = weight.shape[0]
    rank = b_rows.shape[0]
    cols = lambda height: pl.BlockSpec((height, TILE), lambda j, s: (0, j + first))
    own = lambda height: pl.BlockSpec((height, TILE), lambda j, s: (0, j))
    span = (last - first) * TILE
    whole = lambda x: pl.BlockSpec(x.shape, lambda j, s: (0, 0))
    return pl.pallas_call(
        functools.partial(backward_kernel, count, final),
        grid_spec=pltpu.PrefetchScalarGridSpec(
            num_scalar_prefetch=1,
            grid=(last - first,),
            in_specs=[cols(piece)] * (2 * count)
            + [cols(depth), cols(rank), cols(scale8.shape[0])]
            + [whole(live16), whole(live_t), whole(low_t), whole(mask), whole(a_cols)]
            + [whole(x) for x in sums]
            + [pl.BlockSpec(memory_space=pl.ANY)] * len(after),
            out_specs=[
                pl.BlockSpec((rows, depth), lambda j, s: (0, 0)),
                pl.BlockSpec((rows, rank), lambda j, s: (0, 0)),
                own(rank),
                own(live_t.shape[0]),
            ],
            scratch_shapes=([pltpu.VMEM((rows, depth), jnp.float32)] if final else [])
            + [
                pltpu.VMEM((rows, TILE), jnp.bfloat16),
                pltpu.VMEM((rows, TILE), jnp.bfloat16),
            ],
        ),
        out_shape=[
            jax.ShapeDtypeStruct((rows, depth), jnp.bfloat16 if final else jnp.float32),
            jax.ShapeDtypeStruct((rows, rank), jnp.float32),
            jax.ShapeDtypeStruct((rank, span), jnp.float32),
            jax.ShapeDtypeStruct((live_t.shape[0], span), jnp.float32),
        ],
        compiler_params=pltpu.CompilerParams(vmem_limit_bytes=56 * 2**20),
        cost_estimate=pl.CostEstimate(
            flops=2 * rows * depth * span,
            bytes_accessed=2 * (depth * span + 2 * rows * span),
            transcendentals=0,
        ),
    )(places, *grads, *parts, weight, b_rows, scale8, live16, live_t, low_t, mask, a_cols, *sums, *after)


def swap(x, bit):
    return lax.ppermute(x, "inp", [(i, i ^ bit) for i in range(8)])


def swap_sum(x):
    for bit in (1, 2, 4):
        x = x + swap(x, bit)
    return x


def ring(x):
    return lax.ppermute(x, "out", [(i, (i + 1) % 4) for i in range(4)])


def add_bf(a, b):
    return (a.astype(jnp.float32) + b.astype(jnp.float32)).astype(jnp.bfloat16)


def shards_small(
    tokens, weight, adapter_a, adapter_b, magnitude, row_tenant, tenant_count, grad_out
):
    f32, bf16 = jnp.float32, jnp.bfloat16
    highest = lax.Precision.HIGHEST
    contract_rows = (((0,), (0,)), ((), ()))
    tenants, d_local, rank_width = adapter_a.shape
    slots = tenants * rank_width
    f_local = weight.shape[1]
    row_total = row_tenant.shape[0]
    inp_rows = row_total // 8
    out_rows = row_total // 4
    half = inp_rows // 2
    me = lax.axis_index("inp")
    level = lax.axis_index("out")

    X, Y, CORE = 2, 4, 1
    up_a, up_b = grad_out[:half], grad_out[half:]
    ax, by = swap(up_a, X), swap(up_b, Y)
    ay, bx = swap(up_a, Y), swap(up_b, X)
    axy, bxy = swap(ax, Y), swap(by, X)
    same_core = [up_a, up_b, ax, bx, ay, by, axy, bxy]
    grads = same_core + [swap(piece, CORE) for piece in same_core]

    blocks = [tokens]
    for _ in range(3):
        blocks.append(ring(blocks[-1]))
    gathered = jnp.zeros((row_total, d_local), bf16)
    for back, block in enumerate(blocks):
        start = lax.rem(level - back + 4, 4) * out_rows
        gathered = lax.dynamic_update_slice_in_dim(gathered, block, start, 0)

    order = []
    for core in (0, 1):
        for sy, sx in SLOTS:
            for part in (0, 1):
                order.append((me ^ (sy * 4 + sx * 2 + core)) * inp_rows + part * half)
    places = jnp.stack(order).astype(jnp.int32)

    live_table = mask_table(row_tenant, tenant_count)
    slot_mask = jnp.repeat(live_table, rank_width, axis=1)
    a_columns = jnp.transpose(adapter_a, (1, 0, 2)).reshape(d_local, slots)
    b_rows = adapter_b.reshape(slots, f_local)

    b_float = b_rows.astype(f32)
    squares = jnp.sum(jnp.square(weight.astype(f32)), axis=0)
    cross = lax.dot_general(a_columns, weight, contract_rows, preferred_element_type=f32)
    gram = lax.dot_general(a_columns, a_columns, contract_rows, preferred_element_type=f32)
    owner = jnp.arange(slots) // rank_width
    gram = jnp.where(owner[:, None] == owner[None, :], gram, 0.0)
    mixed = 2.0 * cross + jnp.dot(gram, b_float, precision=highest)
    partial_norm = squares[None, :] + jnp.sum(
        (b_float * mixed).reshape(tenants, rank_width, f_local), axis=1
    )
    norm2 = swap_sum(partial_norm)
    inverse = 1.0 / jnp.sqrt(norm2 + epsilon)
    col_scale = magnitude * inverse

    low_part = jnp.dot(gathered, a_columns, preferred_element_type=f32) * slot_mask
    tiles = f_local // TILE
    low_here = low_part.astype(bf16)
    parts = partial_values(
        places, gathered, low_here, weight, b_rows, half, 0, tiles // 2, [ax, by, ay, bx], []
    )
    parts = partial_values(
        places, gathered, low_here, weight, b_rows, half, tiles // 2, tiles, [axy, bxy, *grads[8:14]], parts
    )
    low_t = swap_sum(low_part.T).astype(bf16)

    scale8 = jnp.concatenate([col_scale, jnp.zeros((8 - tenants, f_local), f32)], axis=0)
    live8 = jnp.concatenate([live_table, jnp.zeros((row_total, 8 - tenants), f32)], axis=1)
    live16 = jnp.concatenate([live8, live8], axis=1).astype(bf16)
    live_t = live16.T
    keep, give = parts[:8], parts[8:]
    urgent = (6, 7, 2, 5, 4, 3, 0, 1)
    summed = {}
    for piece in urgent:
        summed[piece] = (keep[piece], swap(give[piece], CORE))
    whole = lambda k: add_bf(*summed[k])
    exact = lambda k: summed[k][0].astype(f32) + summed[k][1].astype(f32)
    ax_far, by_far = swap(whole(6), X), swap(whole(7), Y)
    ax_near, by_near = swap(whole(2), X), swap(whole(5), Y)

    backward = functools.partial(
        backward_parts, places, grads, parts, weight, b_rows, scale8, live16, live_t, low_t, slot_mask, a_columns
    )
    early = backward(0, tiles // 2, [], [summed[6][1], summed[7][1], summed[2][1], summed[5][1]])
    late = backward(tiles // 2, tiles, early[:2], [ax_far, by_far])
    token_part, back_part = late[:2]
    grad_b = jnp.concatenate([early[2], late[2]], axis=1)
    mag_sum = jnp.concatenate([early[3], late[3]], axis=1)[:tenants]
    grad_mag = swap_sum(mag_sum) * inverse

    a_send = (exact(4) + ax_far.astype(f32)).astype(bf16)
    b_send = (exact(3) + by_far.astype(f32)).astype(bf16)
    a_last, b_last = swap(a_send, Y), swap(b_send, X)
    values_a = exact(0) + ax_near.astype(f32) + a_last.astype(f32)
    values_b = exact(1) + by_near.astype(f32) + b_last.astype(f32)
    values = jnp.concatenate([values_a, values_b], axis=0)
    own_live = lax.dynamic_slice_in_dim(live_table, me * inp_rows, inp_rows, 0)
    row_scale = sum(own_live[:, t, None] * col_scale[t, None, :] for t in range(tenants))
    output = (row_scale * values).astype(bf16)

    high = lax.reduce_precision(back_part, 8, 7)
    both = jnp.concatenate([high, back_part - high], axis=1).astype(bf16)
    flat = lax.dot_general(gathered, both, contract_rows, preferred_element_type=f32)
    grad_flat = (flat[:, :slots] + flat[:, slots:]).T
    for bit in (1, 2):
        grad_flat = grad_flat + lax.ppermute(grad_flat, "out", [(i, i ^ bit) for i in range(4)])
    grad_a = jnp.transpose(grad_flat.reshape(tenants, rank_width, d_local), (0, 2, 1))

    def block_of(back):
        start = lax.rem(level - back + 4, 4) * out_rows
        return lax.dynamic_slice_in_dim(token_part, start, out_rows, 0)

    moving = block_of(1)
    for back in (2, 3):
        moving = add_bf(ring(moving), block_of(back))
    grad_tokens = add_bf(ring(moving), block_of(0))
    return (
        output,
        grad_tokens,
        grad_a,
        grad_b.reshape(tenants, rank_width, f_local),
        grad_mag,
    )


def solution(mesh):
    in_specs = (
        P("out", "inp"),
        P("inp", "out"),
        P(None, "inp", None),
        P(None, None, "out"),
        P(None, "out"),
        P(),
        P(),
        P("inp", "out"),
    )
    out_specs = (
        P("inp", "out"),
        P("out", "inp"),
        P(None, "inp", None),
        P(None, None, "out"),
        P(None, "out"),
    )
    small = dict(mesh.shape) == {"inp": 8, "out": 4}
    body = shards_small if small else shards
    return jax.shard_map(body, mesh=mesh, in_specs=in_specs, out_specs=out_specs, check_vma=False)
```
